32 devices in a mesh: bx: 8 (over z, y), by: 4 (over x, core).
Axes of the slice: x: 2, y: 2, z: 4, core: 2. Of those that a mesh axis runs over, the one named last changes fastest.
Arguments:
- views: bfloat16 [4, 512, 256, 128], P(None, ('bx', 'by')), may hold values from 0.25 to 4
- offsets: int32 [4, 2], replicated, may hold values from -16 to 16, as said below
- background: float32 [4], replicated, may hold values from 0.5 to 2
- psf_x: float32 [4, 9], replicated, may hold values from 0.1 to 1
- psf_y: float32 [4, 9], replicated, may hold values from 0.1 to 1
- psf_z: float32 [4, 21], replicated, may hold values from 0.1 to 1
- start: float32 [512, 256, 128], P('bx', 'by'), may hold values from 0.5 to 2
Outputs:
- estimate: float32 [512, 256, 128], P('bx', 'by')
The draws below stay inside these ranges and needn't reach their ends.
Inputs may be any that keep to these rules, and one draw needn't show every extreme that they name: Every offset is nonzero; view 0 has offsets (-16, -16), view 3 has (16, 16), view 1 has a positive first and a negative second offset, view 2 the reverse.
All inputs are finite; a program needn't handle non-finite values.
Results may differ from the reference program's by a relative error of at most 0.0003.
Values may be sent and summed in bfloat16 or wider, within the bound.
A program may use at most 128 MiB of HBM per device.

```python
import math
import jax
import jax.numpy as jnp
from jax import lax

V = 4
SHIFT = 16
KXY = 9
KZ = 21
ITERS = 2
NZ = 128
NX = 512
NY = 256


def draw_offsets(key, part):
    magnitudes = jax.random.randint(key, (V, 2), 1, SHIFT + 1).astype(jnp.int32)
    magnitudes = magnitudes.at[0].set(SHIFT).at[3].set(SHIFT)
    signs = jnp.array([[-1, -1], [1, -1], [-1, 1], [1, 1]], jnp.int32)
    return (magnitudes * signs).astype(jnp.int32)


def shard_levels(key, shape, split, least, top_value):
    def one(axis_at, shards_of):
        steps = jax.random.uniform(jax.random.fold_in(jax.random.fold_in(key, 6), axis_at), (shards_of,), jnp.float32, least / len(split), top_value / len(split))
        return jnp.repeat(jnp.exp(steps), shape[axis_at] // shards_of).reshape((-1,) + (1,) * (len(shape) - axis_at - 1))

    factor_of = one(*split[0])
    for cut in split[1:]:
        factor_of = factor_of * one(*cut)
    return factor_of


def setup_inputs(seed: int = 0) -> dict:
    arg_keys = jax.random.split(jax.random.key(seed), 8)
    return {
        "views": jnp.clip(jnp.exp(math.log(4.0) - 2.7725887 * jax.random.uniform(arg_keys[0], (V, NX, NY, NZ), jnp.float32) ** shard_levels(arg_keys[0], (V, NX, NY, NZ), ((1, 32),), -0.2, 0.2)), 0.25, 4.0).astype(jnp.bfloat16),
        "offsets": draw_offsets(jax.random.fold_in(arg_keys[7], 71), 0),
        "background": jnp.clip(jnp.exp(jax.random.uniform(arg_keys[2], (V,), jnp.float32, math.log(0.5), math.log(2.0))), 0.5, 2.0),
        "psf_x": jnp.clip(jnp.exp(jax.random.uniform(arg_keys[3], (V, KXY), jnp.float32, math.log(0.1), math.log(1.0))), 0.1, 1.0),
        "psf_y": jnp.clip(jnp.exp(jax.random.uniform(arg_keys[4], (V, KXY), jnp.float32, math.log(0.1), math.log(1.0))), 0.1, 1.0),
        "psf_z": jnp.clip(jnp.exp(jax.random.uniform(arg_keys[5], (V, KZ), jnp.float32, math.log(0.1), math.log(1.0))), 0.1, 1.0),
        "start": jnp.clip(jnp.exp(math.log(2.0) - 1.3862944 * jax.random.uniform(arg_keys[6], (NX, NY, NZ), jnp.float32) ** shard_levels(arg_keys[6], (NX, NY, NZ), ((0, 8), (1, 4)), -0.2, 0.2)), 0.5, 2.0),
    }


def depth_band(tap_row, extent):
    length = tap_row.shape[0]
    middle = (length - 1) // 2
    distance = jnp.arange(extent)[:, None] - jnp.arange(extent)[None, :] + middle
    picked = distance[:, :, None] == jnp.arange(length)[None, None, :]
    return jnp.sum(jnp.where(picked, tap_row[None, None, :], 0.0), axis=2)


def along(field, tap_row, axis):
    length = tap_row.shape[0]
    middle = (length - 1) // 2
    extent = field.shape[axis]
    widths = [(0, 0), (0, 0), (0, 0)]
    widths[axis] = (middle, middle)
    padded = jnp.pad(field, widths)
    result = jnp.zeros_like(field)
    for lag_index in range(length):
        result = result + tap_row[lag_index] * lax.slice_in_dim(padded, lag_index, lag_index + extent, axis=axis)
    return result


def forward(field, taps_x, taps_y, taps_z):
    result = along(along(field, taps_x, 0), taps_y, 1)
    return jnp.einsum('xyj,ji->xyi', result, depth_band(taps_z, result.shape[2]), precision=lax.Precision.HIGHEST)


def reference(views, offsets, background, psf_x, psf_y, psf_z, start):
    coord_x = jnp.arange(NX)
    coord_y = jnp.arange(NY)
    weight = jnp.zeros(start.shape, jnp.float32)
    kernels = []
    registered = []
    for which in range(V):
        taps_x = psf_x[which] / jnp.sum(psf_x[which])
        taps_y = psf_y[which] / jnp.sum(psf_y[which])
        taps_z = psf_z[which] / jnp.sum(psf_z[which])
        kernels.append((taps_x, taps_y, taps_z))
        padded = jnp.pad(views[which], ((SHIFT, SHIFT), (SHIFT, SHIFT), (0, 0)))
        moved = lax.dynamic_slice(padded, (SHIFT + offsets[which, 0], SHIFT + offsets[which, 1], jnp.int32(0)), (NX, NY, NZ))
        registered.append(moved)
        inside_x = ((coord_x + offsets[which, 0] >= 0) & (coord_x + offsets[which, 0] < NX)).astype(jnp.float32)
        inside_y = ((coord_y + offsets[which, 1] >= 0) & (coord_y + offsets[which, 1] < NY)).astype(jnp.float32)
        cover = jnp.broadcast_to((inside_x[:, None] * inside_y[None, :])[:, :, None], (NX, NY, NZ))
        weight = weight + forward(cover, taps_x[::-1], taps_y[::-1], taps_z[::-1])
    estimate = start
    for sweep in range(ITERS):
        summed = jnp.zeros(start.shape, jnp.float32)
        for which in range(V):
            taps_x, taps_y, taps_z = kernels[which]
            blurred = forward(estimate, taps_x, taps_y, taps_z)
            ratios = registered[which].astype(jnp.float32) / (blurred + background[which])
            summed = summed + forward(ratios, taps_x[::-1], taps_y[::-1], taps_z[::-1])
        estimate = estimate * summed / weight
    return estimate
```

```python
import functools
import jax
import jax.numpy as jnp
from jax import lax
from jax.experimental import pallas as pl
from jax.experimental.pallas import tpu as pltpu
from jax.sharding import PartitionSpec as P

V = 4
SHIFT = 16
ITERS = 2
H = 4
MESH = pl.DeviceIdType.MESH
F32 = jnp.float32
BF16 = jnp.bfloat16
WAYS = [(1, 0), (-1, 0), (0, 1), (0, -1), (1, 1), (1, -1), (-1, 1), (-1, -1)]


def both(*terms):
    out = terms[0]
    for term in terms[1:]:
        out = jnp.logical_and(out, term)
    return out


def greet(nbx, nby, partners):
    barrier = pltpu.get_barrier_semaphore()
    count = jnp.int32(0)
    for px, py, exists in partners:
        @pl.when(exists)
        def _():
            pl.semaphore_signal(barrier, inc=1, device_id=(px, py), device_id_type=MESH)

        count = count + jnp.where(exists, 1, 0)
    pl.semaphore_wait(barrier, count)


def register_kernel(nbx, nby, blk, rows_y, views, o0, o1, o2, o3, send, recv):
    bx = lax.axis_index("bx")
    by = lax.axis_index("by")
    s = SHIFT // blk
    outs = (o0, o1, o2, o3)
    low = (-s, 0, -s, s)
    count = (nby, nby + s, nby + s, nby)
    left = (-SHIFT, -SHIFT, 0, SHIFT)
    width = (rows_y, rows_y + SHIFT, rows_y + SHIFT, rows_y)
    full = nby * rows_y

    greet(
        nbx,
        nby,
        [
            (bx + dx, jnp.int32(to), both(bx + dx >= 0, bx + dx < nbx, jnp.logical_or(by != to, dx != 0)))
            for dx in (-1, 0, 1)
            for to in range(nby)
        ],
    )

    def columns(view, to):
        first = to * rows_y + left[view]
        begin, end = max(first, 0), min(first + width[view], full)
        return begin, begin - first, end - begin

    def each_send(act):
        for view in range(V):
            for slot, dx in enumerate((-1, 0, 1)):
                k = by - low[view] - nby * dx
                wanted = both(k >= 0, k < count[view], bx + dx >= 0, bx + dx < nbx)
                for step in range(nby):
                    for to in range(nby):
                        turn = lax.rem(by + 1 + step, nby) == to
                        act(view, slot, dx, k, to, both(wanted, turn))

    def start(view, slot, dx, k, to, cond):
        begin, at, wide = columns(view, to)

        def refs():
            row = pl.multiple_of(k * blk, blk)
            return (
                views.at[view, :, pl.ds(begin, wide), :],
                outs[view].at[pl.ds(row, blk), pl.ds(at, wide), :],
            )

        mine = by == to if dx == 0 else None

        @pl.when(cond if mine is None else both(cond, jnp.logical_not(mine)))
        def _():
            src, dst = refs()
            pltpu.make_async_remote_copy(
                src_ref=src,
                dst_ref=dst,
                send_sem=send.at[view, slot, to],
                recv_sem=recv.at[view, k],
                device_id=(bx + dx, jnp.int32(to)),
                device_id_type=MESH,
            ).start()

        if mine is not None:
            @pl.when(both(cond, mine))
            def _():
                src, dst = refs()
                pltpu.make_async_copy(src, dst, recv.at[view, k]).start()

    each_send(start)

    for view in range(V):
        for k in range(count[view]):
            source = nby * bx + low[view] + k
            for to in sorted({0, 1, nby - 1}):
                position = by == to if to in (0, nby - 1) else both(by > 0, by < nby - 1)
                _, at, wide = columns(view, to)

                @pl.when(both(position, source >= 0, source < nbx * nby))
                def _():
                    dst = outs[view].at[pl.ds(k * blk, blk), pl.ds(at, wide), :]
                    pltpu.make_async_copy(dst, dst, recv.at[view, k]).wait()

    for view in range(V):
        for slot, dx in enumerate((-1, 0, 1)):
            k = by - low[view] - nby * dx
            wanted = both(k >= 0, k < count[view], bx + dx >= 0, bx + dx < nbx)
            for to in range(nby):
                cond = both(wanted, by != to) if dx == 0 else wanted
                begin, _, wide = columns(view, to)

                @pl.when(cond)
                def _():
                    src = views.at[view, :, pl.ds(begin, wide), :]
                    pltpu.make_async_copy(src, src, send.at[view, slot, to]).wait()


def deconvolve_kernel(
    nbx, nby, nx, ny, est, reg, tx, ty, bg, wx, planes, band_f, band_t,
    out, E, R, T, U, S, pack, sx, sy, sc, gx, gy, gc, send, recv,
):
    bx = lax.axis_index("bx")
    by = lax.axis_index("by")
    taps = 2 * H + 1
    blocks = nx // 8

    def at(dx, dy):
        return both(bx + dx >= 0, bx + dx < nbx, by + dy >= 0, by + dy < nby)

    greet(nbx, nby, [(bx + dx, by + dy, at(dx, dy)) for dx, dy in WAYS])

    def clear(i, c):
        E[i] = jnp.zeros_like(E[i])
        for v in range(V):
            R[v, i] = jnp.zeros_like(R[v, i])
        return c

    lax.fori_loop(0, nx + 2 * H, clear, 0)

    def message(way, turn, which):
        dx, dy = WAYS[way]
        if dy == 0:
            mine, theirs, n = sx, gx, way
        elif dx == 0:
            mine, theirs, n = sy, gy, way - 2
        else:
            mine, theirs, n = sc, gc, way - 4
        return pltpu.make_async_remote_copy(
            src_ref=mine.at[turn, which, n],
            dst_ref=theirs.at[turn, which, n],
            send_sem=send.at[turn, which, way],
            recv_sem=recv.at[turn, which, way],
            device_id=(bx + dx, by + dy),
            device_id_type=MESH,
        )

    def offer(field, turn, which):
        for n, first in ((0, nx), (1, H)):
            for k in range(H):
                sx[turn, which, n, k * ny : (k + 1) * ny] = field[first + k, 8 : 8 + ny].astype(BF16)

        for n, first in ((0, ny + 8 - H), (1, 8)):
            def rim(i, c):
                for j in range(4):
                    pack[j * H : (j + 1) * H] = field[H + 4 * i + j, first : first + H]
                sy[turn, which, n, pl.ds(pl.multiple_of(16 * i, 16), 16)] = pack[...].astype(BF16)
                return c

            lax.fori_loop(0, nx // 4, rim, 0)
        for n, (dx, dy) in enumerate(WAYS[4:]):
            fx = nx if dx == 1 else H
            fy = ny + 8 - H if dy == 1 else 8
            for k in range(H):
                pack[k * H : (k + 1) * H] = field[fx + k, fy : fy + H]
            sc[turn, which, n] = pack[...].astype(BF16)
        for way, (dx, dy) in enumerate(WAYS):
            @pl.when(at(dx, dy))
            def _():
                message(way, turn, which).start()

    def accept(field, turn, which):
        for way, (dx, dy) in enumerate(WAYS):
            @pl.when(at(-dx, -dy))
            def _():
                message(way, turn, which).wait_recv()
                fx = 0 if dx == 1 else nx + H
                fy = 8 - H if dy == 1 else ny + 8
                if dy == 0:
                    for k in range(H):
                        field[fx + k, 8 : 8 + ny] = gx[turn, which, way, k * ny : (k + 1) * ny].astype(F32)
                elif dx == 0:
                    def rim(i, c):
                        rows = gy[turn, which, way - 2, pl.ds(pl.multiple_of(16 * i, 16), 16)].astype(F32)
                        for j in range(4):
                            field[H + 4 * i + j, fy : fy + H] = rows[j * H : (j + 1) * H]
                        return c

                    lax.fori_loop(0, nx // 4, rim, 0)
                else:
                    rows = gc[turn, which, way - 4].astype(F32)
                    for k in range(H):
                        field[fx + k, fy : fy + H] = rows[k * H : (k + 1) * H]

        for way, (dx, dy) in enumerate(WAYS):
            @pl.when(at(dx, dy))
            def _():
                message(way, turn, which).wait_send()

    def blurred(field, i, ax, ay, band):
        for t in range((ny + 2 * H) // 8):
            rows = [field[8 * i + k, 8 - H + 8 * t : 16 - H + 8 * t] for k in range(7 + taps)]
            for o in range(8):
                acc = ax[0] * rows[o]
                for a in range(1, taps):
                    acc = acc + ax[a] * rows[o + a]
                T[o, 8 * t : 8 * t + 8] = acc
        for o in range(8):
            for t in range(ny // 8):
                acc = ay[0] * T[o, 8 * t : 8 * t + 8]
                for b in range(1, taps):
                    acc = acc + ay[b] * T[o, 8 * t + b : 8 * t + b + 8]
                U[o * ny + 8 * t : o * ny + 8 * t + 8] = acc
        value = U[...]
        high = value.astype(BF16)
        rest = (value - high.astype(F32)).astype(BF16)
        return jnp.dot(
            jnp.concatenate([high, rest, high], axis=1), band, preferred_element_type=F32
        )

    def load(i, c):
        E[H + i, 8 : 8 + ny] = est[i]
        return c

    lax.fori_loop(0, nx, load, 0)

    def sweep(turn, c):
        offer(E, turn, V)
        accept(E, turn, V)

        def ahead(v, c):
            ax = [tx[v, a] for a in range(taps)]
            ay = [ty[v, a] for a in range(taps)]
            base = bg[v]

            def block(i, c):
                got = blurred(E, i, ax, ay, band_f[v])
                for o in range(8):
                    R[v, H + 8 * i + o, 8 : 8 + ny] = reg[v, 8 * i + o].astype(F32) / (
                        got[o * ny : (o + 1) * ny] + base
                    )
                return c

            lax.fori_loop(0, blocks, block, 0)
            offer(R.at[v], turn, v)
            return c

        lax.fori_loop(0, V, ahead, 0)

        def back(v, c):
            accept(R.at[v], turn, v)
            ax = [tx[v, taps - 1 - a] for a in range(taps)]
            ay = [ty[v, taps - 1 - a] for a in range(taps)]
            keep = jnp.where(v == 0, 0.0, 1.0).astype(F32)

            def block(i, c):
                got = blurred(R.at[v], i, ax, ay, band_t[v])
                for o in range(8):
                    S[8 * i + o] = S[8 * i + o] * keep + got[o * ny : (o + 1) * ny]
                return c

            lax.fori_loop(0, blocks, block, 0)
            return c

        def empty(i, c):
            S[i] = jnp.zeros_like(S[i])
            return c

        lax.fori_loop(0, nx, empty, 0)
        lax.fori_loop(0, V, back, 0)

        def update(i, c):
            weight = wx[0, i] * planes[0]
            for v in range(1, V):
                weight = weight + wx[v, i] * planes[v]
            E[H + i, 8 : 8 + ny] = E[H + i, 8 : 8 + ny] * S[i] / weight
            return c

        lax.fori_loop(0, nx, update, 0)
        return c

    lax.fori_loop(0, ITERS, sweep, 0)

    def store(i, c):
        out[i] = E[H + i, 8 : 8 + ny]
        return c

    lax.fori_loop(0, nx, store, 0)


def band_rows(tap_row, extent):
    length = tap_row.shape[0]
    distance = jnp.arange(extent + length - 1)[None, :] - jnp.arange(extent)[:, None]
    picked = distance[:, :, None] == jnp.arange(length)[None, None, :]
    return jnp.sum(jnp.where(picked, tap_row[None, None, :], 0.0), axis=2)


def depth_bands(taps, extent):
    length = taps.shape[1]
    middle = (length - 1) // 2
    distance = jnp.arange(extent)[:, None] - jnp.arange(extent)[None, :] + middle
    band = jnp.zeros((taps.shape[0], extent, extent), F32)
    for lag in range(length):
        band = jnp.where(distance[None] == lag, taps[:, lag, None, None], band)
    return band


def stacked(band):
    high = band.astype(BF16)
    rest = (band - high.astype(F32)).astype(BF16)
    return jnp.concatenate([high, high, rest], axis=1)


def local(views, offsets, background, psf_x, psf_y, psf_z, start):
    rows_x, rows_y, depth = start.shape
    nbx = lax.axis_size("bx")
    nby = lax.axis_size("by")
    full_x = rows_x * nbx
    full_y = rows_y * nby
    blk = views.shape[1]
    middle = (psf_x.shape[1] - 1) // 2
    spread = SHIFT // blk
    vmem = pl.BlockSpec(memory_space=pltpu.VMEM)
    smem = pl.BlockSpec(memory_space=pltpu.SMEM)
    anywhere = pl.BlockSpec(memory_space=pl.ANY)

    moved = pl.pallas_call(
        functools.partial(register_kernel, nbx, nby, blk, rows_y),
        out_shape=[
            jax.ShapeDtypeStruct((rows_x, rows_y, depth), BF16),
            jax.ShapeDtypeStruct((rows_x + SHIFT, rows_y + SHIFT, depth), BF16),
            jax.ShapeDtypeStruct((rows_x + SHIFT, rows_y + SHIFT, depth), BF16),
            jax.ShapeDtypeStruct((rows_x, rows_y, depth), BF16),
        ],
        in_specs=[anywhere],
        out_specs=[anywhere] * 4,
        scratch_shapes=[
            pltpu.SemaphoreType.DMA((V, 3, nby)),
            pltpu.SemaphoreType.DMA((V, nby + spread)),
        ],
        compiler_params=pltpu.CompilerParams(collective_id=0, has_side_effects=True),
    )(views)

    taps_x = psf_x / jnp.sum(psf_x, axis=1, keepdims=True)
    taps_y = psf_y / jnp.sum(psf_y, axis=1, keepdims=True)
    taps_z = psf_z / jnp.sum(psf_z, axis=1, keepdims=True)
    at_x = lax.axis_index("bx") * rows_x - middle + jnp.arange(rows_x + 2 * middle, dtype=jnp.int32)
    at_y = lax.axis_index("by") * rows_y - middle + jnp.arange(rows_y + 2 * middle, dtype=jnp.int32)

    def covered(at, shift, full):
        there = at[None, :] + shift[:, None]
        return (at >= 0) & (at < full) & (there >= 0) & (there < full)

    cover_x = covered(at_x, offsets[:, 0], full_x)
    cover_y = covered(at_y, offsets[:, 1], full_y)

    def folded(cover, taps, rows):
        total = jnp.zeros((V, rows), F32)
        for lag in range(2 * middle + 1):
            total = total + taps[:, 2 * middle - lag, None] * cover[:, lag : lag + rows].astype(F32)
        return total

    weight_x = folded(cover_x, taps_x, rows_x)
    weight_y = folded(cover_y, taps_y, rows_y)
    band_f = depth_bands(taps_z, depth)
    band_t = depth_bands(taps_z[:, ::-1], depth)
    weight_z = jnp.sum(band_t, axis=1)
    planes = weight_y[:, :, None] * weight_z[:, None, :]

    zero = jnp.zeros((), jnp.int32)
    size = (rows_x, rows_y, depth)
    cut = [
        moved[0],
        lax.dynamic_slice(moved[1], (offsets[1, 0], SHIFT + offsets[1, 1], zero), size),
        lax.dynamic_slice(moved[2], (SHIFT + offsets[2, 0], offsets[2, 1], zero), size),
        moved[3],
    ]
    inner_x = cover_x[:, middle : middle + rows_x]
    inner_y = cover_y[:, middle : middle + rows_y]
    registered = jnp.stack(
        [
            jnp.where(inner_x[v][:, None, None] & inner_y[v][None, :, None], cut[v], jnp.zeros((), BF16))
            for v in range(V)
        ]
    )

    rim_x = H * rows_y
    rim_y = H * rows_x
    return pl.pallas_call(
        functools.partial(deconvolve_kernel, nbx, nby, rows_x, rows_y),
        out_shape=jax.ShapeDtypeStruct(start.shape, F32),
        in_specs=[vmem, vmem, smem, smem, smem, smem, vmem, vmem, vmem],
        out_specs=vmem,
        scratch_shapes=[
            pltpu.VMEM((rows_x + 2 * H, rows_y + 16, depth), F32),
            pltpu.VMEM((V, rows_x + 2 * H, rows_y + 16, depth), F32),
            pltpu.VMEM((8, rows_y + 2 * H, depth), F32),
            pltpu.VMEM((8 * rows_y, depth), F32),
            pltpu.VMEM(start.shape, F32),
            pltpu.VMEM((16, depth), F32),
            pltpu.VMEM((ITERS, V + 1, 2, rim_x, depth), BF16),
            pltpu.VMEM((ITERS, V + 1, 2, rim_y, depth), BF16),
            pltpu.VMEM((ITERS, V + 1, 4, 16, depth), BF16),
            pltpu.VMEM((ITERS, V + 1, 2, rim_x, depth), BF16),
            pltpu.VMEM((ITERS, V + 1, 2, rim_y, depth), BF16),
            pltpu.VMEM((ITERS, V + 1, 4, 16, depth), BF16),
            pltpu.SemaphoreType.DMA((ITERS, V + 1, 8)),
            pltpu.SemaphoreType.DMA((ITERS, V + 1, 8)),
        ],
        compiler_params=pltpu.CompilerParams(
            collective_id=1, has_side_effects=True, vmem_limit_bytes=56 * 1024 * 1024
        ),
    )(start, registered, taps_x, taps_y, background, weight_x, planes, stacked(band_f), stacked(band_t))


def solution(mesh):
    return jax.shard_map(
        local,
        mesh=mesh,
        in_specs=(P(None, ("bx", "by"), None, None), P(), P(), P(), P(), P(), P("bx", "by", None)),
        out_specs=P("bx", "by", None),
        check_vma=False,
    )
```

```python
import functools
import jax
import jax.numpy as jnp
from jax import lax
from jax.experimental import pallas as pl
from jax.experimental.pallas import tpu as pltpu
from jax.sharding import PartitionSpec as P

V = 4
SHIFT = 16
ITERS = 2
H = 4
MESH = pl.DeviceIdType.MESH
F32 = jnp.float32
BF16 = jnp.bfloat16
WAYS = [(1, 0), (-1, 0), (0, 1), (0, -1), (1, 1), (1, -1), (-1, 1), (-1, -1)]


def both(*terms):
    out = terms[0]
    for term in terms[1:]:
        out = jnp.logical_and(out, term)
    return out


def greet(nbx, nby, partners):
    barrier = pltpu.get_barrier_semaphore()
    count = jnp.int32(0)
    for px, py, exists in partners:
        @pl.when(exists)
        def _():
            pl.semaphore_signal(barrier, inc=1, device_id=(px, py), device_id_type=MESH)

        count = count + jnp.where(exists, 1, 0)
    pl.semaphore_wait(barrier, count)


def deconvolve_kernel(
    nbx, nby, nx, ny, blk, depth,
    views, start, taps, offsets, bg,
    out, r0, r1, r2, r3, E, inverse, Eb, Rb, halo, rim, G, U, ratio, pack, LF, LT, ZF, ZT, pick, planes, WX,
    send_v, recv_v, send, recv,
):
    bx = lax.axis_index("bx")
    by = lax.axis_index("by")
    kxy = 2 * H + 1
    kz = taps.shape[1] - 2 * kxy
    blocks = nx // 8
    s = SHIFT // blk
    regs = (r0, r1, r2, r3)
    low = (-s, 0, -s, s)
    count = (nby, nby + s, nby + s, nby)
    left = (-SHIFT, -SHIFT, 0, SHIFT)
    width = (ny, ny + SHIFT, ny + SHIFT, ny)
    full = nby * ny

    def at(dx, dy):
        return both(bx + dx >= 0, bx + dx < nbx, by + dy >= 0, by + dy < nby)

    def columns(view, to):
        first = to * ny + left[view]
        begin, end = max(first, 0), min(first + width[view], full)
        return begin, begin - first, end - begin

    def row_block(view, dx):
        k = by - low[view] - nby * dx
        return k, both(k >= 0, k < count[view], bx + dx >= 0, bx + dx < nbx)

    def start_view(view, slot, dx, k, to, cond):
        begin, at_y, wide = columns(view, to)

        def refs():
            row = pl.multiple_of(k * blk, blk)
            return (
                views.at[view, :, pl.ds(begin, wide), :],
                regs[view].at[pl.ds(row, blk), pl.ds(at_y, wide), :],
            )

        mine = by == to if dx == 0 else None

        @pl.when(cond if mine is None else both(cond, jnp.logical_not(mine)))
        def _():
            src, dst = refs()
            pltpu.make_async_remote_copy(
                src_ref=src,
                dst_ref=dst,
                send_sem=send_v.at[view, slot, to],
                recv_sem=recv_v.at[view, k],
                device_id=(bx + dx, jnp.int32(to)),
                device_id_type=MESH,
            ).start()

        if mine is not None:
            @pl.when(both(cond, mine))
            def _():
                src, dst = refs()
                pltpu.make_async_copy(src, dst, recv_v.at[view, k]).start()

    def start_views():
        for view in range(V):
            for slot, dx in enumerate((-1, 0, 1)):
                k, wanted = row_block(view, dx)
                for step in range(nby):
                    for to in range(nby):
                        turn = lax.rem(by + 1 + step, nby) == to
                        start_view(view, slot, dx, k, to, both(wanted, turn))

    def accept_view(view):
        for k in range(count[view]):
            source = nby * bx + low[view] + k
            for to in sorted({0, 1, nby - 1}):
                position = by == to if to in (0, nby - 1) else both(by > 0, by < nby - 1)
                _, at_y, wide = columns(view, to)

                @pl.when(both(position, source >= 0, source < nbx * nby))
                def _():
                    dst = regs[view].at[pl.ds(k * blk, blk), pl.ds(at_y, wide), :]
                    pltpu.make_async_copy(dst, dst, recv_v.at[view, k]).wait()

    def finish_views():
        for view in range(V):
            for slot, dx in enumerate((-1, 0, 1)):
                k, wanted = row_block(view, dx)
                for to in range(nby):
                    begin, _, wide = columns(view, to)

                    @pl.when(both(wanted, by != to) if dx == 0 else wanted)
                    def _():
                        src = views.at[view, :, pl.ds(begin, wide), :]
                        pltpu.make_async_copy(src, src, send_v.at[view, slot, to]).wait()

    def message(field, turn, which, way):
        dx, dy = WAYS[way]
        side = 0 if dy == 1 else 1
        if dy == 0:
            src = field.at[pl.ds(nx if dx == 1 else H, H)]
            dst = field.at[pl.ds(0 if dx == 1 else nx + H, H)]
        elif dx == 0:
            src = rim.at[turn, which, side]
            dst = halo.at[turn, which, side, pl.ds(16, 4 * nx)]
        else:
            src = rim.at[turn, which, side, pl.ds(4 * nx - 16 if dx == 1 else 0, 16)]
            dst = halo.at[turn, which, side, pl.ds(0 if dx == 1 else 4 * nx + 16, 16)]
        return pltpu.make_async_remote_copy(
            src_ref=src,
            dst_ref=dst,
            send_sem=send.at[turn, which, way],
            recv_sem=recv.at[turn, which, way],
            device_id=(bx + dx, by + dy),
            device_id_type=MESH,
        )

    def offer(field, turn, which):
        for way, (dx, dy) in enumerate(WAYS):
            @pl.when(at(dx, dy))
            def _():
                message(field, turn, which, way).start()

    def accept(field, turn, which):
        for way, (dx, dy) in enumerate(WAYS):
            @pl.when(at(-dx, -dy))
            def _():
                message(field, turn, which, way).wait_recv()

    def finish(field, turn, which):
        for way, (dx, dy) in enumerate(WAYS):
            @pl.when(at(dx, dy))
            def _():
                message(field, turn, which, way).wait_send()

    def pack_rim(source, turn, which, i):
        for o in range(8):
            row = source(o)
            pack[0, o * H : (o + 1) * H] = row[ny - H : ny]
            pack[1, o * H : (o + 1) * H] = row[0:H]
        for side in range(2):
            rim[turn, which, side, pl.ds(pl.multiple_of(32 * i, 32), 32)] = pack[side].astype(BF16)

    def publish(turn):
        def block(i, c):
            for o in range(8):
                Eb[turn, H + 8 * i + o] = E[8 * i + o].astype(BF16)
            pack_rim(lambda o: E.at[8 * i + o], turn, V, i)
            return c

        lax.fori_loop(0, blocks, block, 0)

    def clear_small(i, c):
        r0[i] = jnp.zeros((ny, depth), BF16)
        r3[i] = jnp.zeros((ny, depth), BF16)
        E[i] = start[i]
        return c

    def clear_large(i, c):
        r1[i] = jnp.zeros((ny + SHIFT, depth), BF16)
        r2[i] = jnp.zeros((ny + SHIFT, depth), BF16)
        return c

    lax.fori_loop(0, nx, clear_small, 0)
    lax.fori_loop(0, nx + SHIFT, clear_large, 0)
    for turn in range(ITERS):
        for k in range(H):
            for first in (0, nx + H):
                Eb[turn, first + k] = jnp.zeros((ny, depth), BF16)
                for v in range(V):
                    Rb[turn, v, first + k] = jnp.zeros((ny, depth), BF16)

        def clear_halo(which, c):
            for side in range(2):
                halo[turn, which, side] = jnp.zeros((4 * nx + 32, depth), BF16)
            return c

        lax.fori_loop(0, V + 1, clear_halo, 0)
    publish(0)

    greet(
        nbx,
        nby,
        [
            (bx + dx, jnp.int32(to), both(bx + dx >= 0, bx + dx < nbx, jnp.logical_or(by != to, dx != 0)))
            for dx in (-1, 0, 1)
            for to in range(nby)
        ],
    )
    offer(Eb.at[0], 0, V)
    start_views()

    def split(band):
        high = band.astype(BF16)
        return high, (band - high.astype(F32)).astype(BF16)

    row = lax.broadcasted_iota(jnp.int32, (ny, 128), 0)
    col = lax.broadcasted_iota(jnp.int32, (ny, 128), 1)
    inside = col < ny
    second = col >= ny + 16
    place = jnp.where(inside, col, jnp.where(second, ny + (col & 3), (col & 3) - H))
    owner = jnp.where(inside, -1, (col & 15) >> 2)
    lag_y = place - row + H
    z_in = lax.broadcasted_iota(jnp.int32, (depth, depth), 0)
    z_out = lax.broadcasted_iota(jnp.int32, (depth, depth), 1)
    lag_z = z_in - z_out + (kz - 1) // 2

    def build(v, c):
        forth = jnp.zeros((ny, 128), F32)
        back = jnp.zeros((ny, 128), F32)
        for b in range(kxy):
            forth = jnp.where(lag_y == b, taps[v, kxy + b], forth)
            back = jnp.where(lag_y == b, taps[v, 2 * kxy - 1 - b], back)
        for j in range(4):
            used = jnp.logical_and(
                jnp.logical_or(owner == -1, owner == j), col < ny + 32
            )
            for side, (target, band) in enumerate(((LF, forth), (LT, back))):
                high, rest = split(jnp.where(used, band, 0.0))
                base = pl.multiple_of(v * ny, ny)
                target[j, pl.ds(base, ny), 0:128] = high
                target[j, pl.ds(base, ny), 128:256] = rest
        forth = jnp.zeros((depth, depth), F32)
        back = jnp.zeros((depth, depth), F32)
        for b in range(kz):
            forth = jnp.where(lag_z == b, taps[v, 2 * kxy + b], forth)
            back = jnp.where(lag_z == b, taps[v, 2 * kxy + kz - 1 - b], back)
        for target, band in ((ZF, forth), (ZT, back)):
            high, rest = split(band)
            base = pl.multiple_of(v * 3 * depth, 3 * depth)
            target[pl.ds(base, depth)] = high
            target[pl.ds(base + depth, depth)] = high
            target[pl.ds(base + 2 * depth, depth)] = rest
        weight_z = jnp.sum(back, axis=0, keepdims=True)

        def folded(first, shift, limit, base, rows):
            total = jnp.zeros((rows, 128), F32)
            cell = first - H + lax.broadcasted_iota(jnp.int32, (rows, 128), 0)
            for b in range(kxy):
                here = cell + b
                there = here + shift
                good = both(here >= 0, here < limit, there >= 0, there < limit)
                total = total + jnp.where(good, taps[v, base + kxy - 1 - b], 0.0)
            return total

        planes[v] = folded(by * ny, offsets[v, 1], nby * ny, kxy, ny) * weight_z
        WX[v] = folded(bx * nx, offsets[v, 0], nbx * nx, 0, nx)
        return c

    lax.fori_loop(0, V, build, 0)

    pick_row = lax.broadcasted_iota(jnp.int32, (ny, ny + SHIFT), 0)
    pick_col = lax.broadcasted_iota(jnp.int32, (ny, ny + SHIFT), 1)
    for n, shift in enumerate((SHIFT + offsets[1, 1], offsets[2, 1])):
        pick[n] = jnp.where(pick_col == pick_row + shift, 1.0, 0.0).astype(BF16)

    def invert(i, c):
        rows = [WX[v, pl.ds(pl.multiple_of(8 * i, 8), 8)] for v in range(V)]
        for o in range(8):
            weight = rows[0][o : o + 1] * planes[0]
            for v in range(1, V):
                weight = weight + rows[v][o : o + 1] * planes[v]
            inverse[8 * i + o] = 1.0 / weight
        return c

    lax.fori_loop(0, blocks, invert, 0)

    def column(field, turn, which, q, j):
        tile = pl.ds(pl.multiple_of(16 * q, 16), 16)
        once = [
            field[4 * q + j],
            halo[turn, which, 0, tile],
            halo[turn, which, 1, tile],
            jnp.zeros((128 - ny - 32, depth), BF16),
        ]
        return jnp.concatenate(once + once, axis=0)

    def along_x(v, i, reverse):
        weights = [taps[v, kxy - 1 - a if reverse else a] for a in range(kxy)]
        for t in range(0, ny, 16):
            halves = []
            for u in (t, t + 8):
                rows = [G[v, 8 * i + k, u : u + 8] for k in range(7 + kxy)]
                sums = []
                for o in range(8):
                    acc = weights[0] * rows[o]
                    for a in range(1, kxy):
                        acc = acc + weights[a] * rows[o + a]
                    sums.append(acc)
                halves.append(sums)
            for o in range(8):
                both_halves = jnp.concatenate([halves[0][o], halves[1][o]], axis=0)
                high, rest = split(both_halves)
                U[v, o * ny + t : o * ny + t + 16, :depth] = high
                U[v, o * ny + t : o * ny + t + 16, depth:] = rest

    def sweep(turn, c):
        accept(Eb.at[turn], turn, V)

        def all_views(q, c):
            for j in range(4):
                got = jnp.dot(
                    LF[j], column(Eb.at[turn], turn, V, q, j), preferred_element_type=F32
                )
                for v in range(V):
                    G[v, 4 * q + j] = got[v * ny : (v + 1) * ny]
            return c

        lax.fori_loop(0, (nx + 2 * H) // 4, all_views, 0)

        for v in range(V):
            @pl.when(turn == 0)
            def _():
                accept_view(v)

            first_x = {1: offsets[1, 0], 2: SHIFT + offsets[2, 0]}.get(v, 0)

            def ahead(i, c):
                along_x(v, i, False)
                got = jnp.dot(
                    jnp.concatenate([U[v], U[v, :, :depth]], axis=1),
                    ZF[3 * v * depth : 3 * (v + 1) * depth],
                    preferred_element_type=F32,
                )
                for o in range(8):
                    if v in (1, 2):
                        seen = jnp.dot(
                            pick[v - 1], regs[v][first_x + 8 * i + o], preferred_element_type=F32
                        )
                    else:
                        seen = regs[v][8 * i + o].astype(F32)
                    value = seen / (got[o * ny : (o + 1) * ny] + bg[v])
                    Rb[turn, v, H + 8 * i + o] = value.astype(BF16)
                    ratio[o] = value
                pack_rim(lambda o: ratio.at[o], turn, v, i)
                return c

            lax.fori_loop(0, blocks, ahead, 0)
            offer(Rb.at[turn, v], turn, v)

        def back(v, c):
            accept(Rb.at[turn, v], turn, v)

            def one_view(q, c):
                for j in range(4):
                    G[v, 4 * q + j] = jnp.dot(
                        LT[j, pl.ds(pl.multiple_of(v * ny, ny), ny)],
                        column(Rb.at[turn, v], turn, v, q, j),
                        preferred_element_type=F32,
                    )
                return c

            lax.fori_loop(0, (nx + 2 * H) // 4, one_view, 0)
            return c

        lax.fori_loop(0, V, back, 0)

        def update(i, c):
            for v in range(V):
                along_x(v, i, True)
            got = jnp.dot(
                jnp.concatenate(
                    [part for v in range(V) for part in (U[v], U[v, :, :depth])], axis=1
                ),
                ZT[...],
                preferred_element_type=F32,
            )
            for o in range(8):
                x = 8 * i + o
                E[x] = E[x] * got[o * ny : (o + 1) * ny] * inverse[x]
            return c

        lax.fori_loop(0, blocks, update, 0)

        finish(Eb.at[turn], turn, V)
        for v in range(V):
            finish(Rb.at[turn, v], turn, v)

        @pl.when(turn < ITERS - 1)
        def _():
            publish(turn + 1)
            offer(Eb.at[turn + 1], turn + 1, V)

        return c

    lax.fori_loop(0, ITERS, sweep, 0)
    finish_views()

    def store(i, c):
        out[i] = E[i]
        return c

    lax.fori_loop(0, nx, store, 0)


def local(views, offsets, background, psf_x, psf_y, psf_z, start):
    rows_x, rows_y, depth = start.shape
    nbx = lax.axis_size("bx")
    nby = lax.axis_size("by")
    blk = views.shape[1]
    vmem = pl.BlockSpec(memory_space=pltpu.VMEM)
    smem = pl.BlockSpec(memory_space=pltpu.SMEM)
    anywhere = pl.BlockSpec(memory_space=pl.ANY)
    taps = jnp.concatenate([p / jnp.sum(p, axis=1, keepdims=True) for p in (psf_x, psf_y, psf_z)], axis=1)
    tall = rows_x + 2 * H
    small = (rows_x, rows_y, depth)
    large = (rows_x + SHIFT, rows_y + SHIFT, depth)
    return pl.pallas_call(
        functools.partial(deconvolve_kernel, nbx, nby, rows_x, rows_y, blk, depth),
        out_shape=jax.ShapeDtypeStruct(start.shape, F32),
        in_specs=[anywhere, vmem, smem, smem, smem],
        out_specs=vmem,
        scratch_shapes=[
            pltpu.VMEM(small, BF16),
            pltpu.VMEM(large, BF16),
            pltpu.VMEM(large, BF16),
            pltpu.VMEM(small, BF16),
            pltpu.VMEM(small, F32),
            pltpu.VMEM(small, F32),
            pltpu.VMEM((ITERS, tall, rows_y, depth), BF16),
            pltpu.VMEM((ITERS, V, tall, rows_y, depth), BF16),
            pltpu.VMEM((ITERS, V + 1, 2, H * tall, depth), BF16),
            pltpu.VMEM((ITERS, V + 1, 2, H * rows_x, depth), BF16),
            pltpu.VMEM((V, tall, rows_y, depth), F32),
            pltpu.VMEM((V, 8 * rows_y, 2 * depth), BF16),
            pltpu.VMEM((8, rows_y, depth), F32),
            pltpu.VMEM((2, 32, depth), F32),
            pltpu.VMEM((4, V * rows_y, 256), BF16),
            pltpu.VMEM((4, V * rows_y, 256), BF16),
            pltpu.VMEM((3 * V * depth, depth), BF16),
            pltpu.VMEM((3 * V * depth, depth), BF16),
            pltpu.VMEM((2, rows_y, rows_y + SHIFT), BF16),
            pltpu.VMEM((V, rows_y, depth), F32),
            pltpu.VMEM((V, rows_x, depth), F32),
            pltpu.SemaphoreType.DMA((V, 3, nby)),
            pltpu.SemaphoreType.DMA((V, nby + SHIFT // blk)),
            pltpu.SemaphoreType.DMA((ITERS, V + 1, 8)),
            pltpu.SemaphoreType.DMA((ITERS, V + 1, 8)),
        ],
        compiler_params=pltpu.CompilerParams(
            collective_id=0, has_side_effects=True, vmem_limit_bytes=56 * 1024 * 1024
        ),
    )(views, start, taps, offsets, background)


def solution(mesh):
    return jax.shard_map(
        local,
        mesh=mesh,
        in_specs=(P(None, ("bx", "by"), None, None), P(), P(), P(), P(), P(), P("bx", "by", None)),
        out_specs=P("bx", "by", None),
        check_vma=False,
    )
```

```python
import functools
import jax
import jax.numpy as jnp
from jax import lax
from jax.experimental import pallas as pl
from jax.experimental.pallas import tpu as pltpu
from jax.sharding import PartitionSpec as P

V = 4
SHIFT = 16
ITERS = 2
H = 4
MESH = pl.DeviceIdType.MESH
F32 = jnp.float32
BF16 = jnp.bfloat16
WAYS = [(1, 0), (-1, 0), (0, 1), (0, -1), (1, 1), (1, -1), (-1, 1), (-1, -1)]


def both(*terms):
    out = terms[0]
    for term in terms[1:]:
        out = jnp.logical_and(out, term)
    return out


def greet(nbx, nby, partners):
    barrier = pltpu.get_barrier_semaphore()
    count = jnp.int32(0)
    for px, py, exists in partners:
        @pl.when(exists)
        def _():
            pl.semaphore_signal(barrier, inc=1, device_id=(px, py), device_id_type=MESH)

        count = count + jnp.where(exists, 1, 0)
    pl.semaphore_wait(barrier, count)


def deconvolve_kernel(
    nbx, nby, nx, ny, blk, depth,
    views, start, taps, offsets, bg,
    out, r0, r1, r2, r3, E, inverse, Eb, Rb, halo, rim, G, U, D, ratio, pack, LF, LT, ZF, ZT, pick, planes, WX,
    send_v, recv_v, send, recv,
):
    bx = lax.axis_index("bx")
    by = lax.axis_index("by")
    kxy = 2 * H + 1
    kz = taps.shape[1] - 2 * kxy
    blocks = nx // 8
    s = SHIFT // blk
    regs = (r0, r1, r2, r3)
    low = (-s, 0, -s, s)
    count = (nby, nby + s, nby + s, nby)
    left = (-SHIFT, -SHIFT, 0, SHIFT)
    width = (ny, ny + SHIFT, ny + SHIFT, ny)
    full = nby * ny

    def at(dx, dy):
        return both(bx + dx >= 0, bx + dx < nbx, by + dy >= 0, by + dy < nby)

    def columns(view, to):
        first = to * ny + left[view]
        begin, end = max(first, 0), min(first + width[view], full)
        return begin, begin - first, end - begin

    def row_block(view, dx):
        k = by - low[view] - nby * dx
        return k, both(k >= 0, k < count[view], bx + dx >= 0, bx + dx < nbx)

    def start_view(view, slot, dx, k, to, cond):
        begin, at_y, wide = columns(view, to)

        def refs():
            row = pl.multiple_of(k * blk, blk)
            return (
                views.at[view, :, pl.ds(begin, wide), :],
                regs[view].at[pl.ds(row, blk), pl.ds(at_y, wide), :],
            )

        mine = by == to if dx == 0 else None

        @pl.when(cond if mine is None else both(cond, jnp.logical_not(mine)))
        def _():
            src, dst = refs()
            pltpu.make_async_remote_copy(
                src_ref=src,
                dst_ref=dst,
                send_sem=send_v.at[view, slot, to],
                recv_sem=recv_v.at[view, k],
                device_id=(bx + dx, jnp.int32(to)),
                device_id_type=MESH,
            ).start()

        if mine is not None:
            @pl.when(both(cond, mine))
            def _():
                src, dst = refs()
                pltpu.make_async_copy(src, dst, recv_v.at[view, k]).start()

    def start_views():
        for view in range(V):
            for slot, dx in enumerate((-1, 0, 1)):
                k, wanted = row_block(view, dx)
                for step in range(nby):
                    for to in range(nby):
                        turn = lax.rem(by + 1 + step, nby) == to
                        start_view(view, slot, dx, k, to, both(wanted, turn))

    def accept_view(view):
        for k in range(count[view]):
            source = nby * bx + low[view] + k
            for to in sorted({0, 1, nby - 1}):
                position = by == to if to in (0, nby - 1) else both(by > 0, by < nby - 1)
                _, at_y, wide = columns(view, to)

                @pl.when(both(position, source >= 0, source < nbx * nby))
                def _():
                    dst = regs[view].at[pl.ds(k * blk, blk), pl.ds(at_y, wide), :]
                    pltpu.make_async_copy(dst, dst, recv_v.at[view, k]).wait()

    def finish_views():
        for view in range(V):
            for slot, dx in enumerate((-1, 0, 1)):
                k, wanted = row_block(view, dx)
                for to in range(nby):
                    begin, _, wide = columns(view, to)

                    @pl.when(both(wanted, by != to) if dx == 0 else wanted)
                    def _():
                        src = views.at[view, :, pl.ds(begin, wide), :]
                        pltpu.make_async_copy(src, src, send_v.at[view, slot, to]).wait()

    def message(field, turn, which, way):
        dx, dy = WAYS[way]
        side = 0 if dy == 1 else 1
        if dy == 0:
            src = field.at[pl.ds(nx if dx == 1 else H, H)]
            dst = field.at[pl.ds(0 if dx == 1 else nx + H, H)]
        elif dx == 0:
            src = rim.at[turn, which, side]
            dst = halo.at[turn, which, side, pl.ds(16, 4 * nx)]
        else:
            src = rim.at[turn, which, side, pl.ds(4 * nx - 16 if dx == 1 else 0, 16)]
            dst = halo.at[turn, which, side, pl.ds(0 if dx == 1 else 4 * nx + 16, 16)]
        return pltpu.make_async_remote_copy(
            src_ref=src,
            dst_ref=dst,
            send_sem=send.at[turn, which, way],
            recv_sem=recv.at[turn, which, way],
            device_id=(bx + dx, by + dy),
            device_id_type=MESH,
        )

    def offer(field, turn, which):
        for way, (dx, dy) in enumerate(WAYS):
            @pl.when(at(dx, dy))
            def _():
                message(field, turn, which, way).start()

    def accept(field, turn, which):
        for way, (dx, dy) in enumerate(WAYS):
            @pl.when(at(-dx, -dy))
            def _():
                message(field, turn, which, way).wait_recv()

    def finish(field, turn, which):
        for way, (dx, dy) in enumerate(WAYS):
            @pl.when(at(dx, dy))
            def _():
                message(field, turn, which, way).wait_send()

    def pack_rim(source, turn, which, i):
        for o in range(8):
            row = source(o)
            pack[0, o * H : (o + 1) * H] = row[ny - H : ny]
            pack[1, o * H : (o + 1) * H] = row[0:H]
        for side in range(2):
            rim[turn, which, side, pl.ds(pl.multiple_of(32 * i, 32), 32)] = pack[side].astype(BF16)

    def publish(turn):
        def block(i, c):
            for o in range(8):
                Eb[turn, H + 8 * i + o] = E[8 * i + o].astype(BF16)
            pack_rim(lambda o: E.at[8 * i + o], turn, V, i)
            return c

        lax.fori_loop(0, blocks, block, 0)

    def clear_small(i, c):
        r0[i] = jnp.zeros((ny, depth), BF16)
        r3[i] = jnp.zeros((ny, depth), BF16)
        E[i] = start[i]
        return c

    def clear_large(i, c):
        r1[i] = jnp.zeros((ny + SHIFT, depth), BF16)
        r2[i] = jnp.zeros((ny + SHIFT, depth), BF16)
        return c

    lax.fori_loop(0, nx, clear_small, 0)
    lax.fori_loop(0, nx + SHIFT, clear_large, 0)
    for turn in range(ITERS):
        for k in range(H):
            for first in (0, nx + H):
                Eb[turn, first + k] = jnp.zeros((ny, depth), BF16)
                for v in range(V):
                    Rb[turn, v, first + k] = jnp.zeros((ny, depth), BF16)

        def clear_halo(which, c):
            for side in range(2):
                halo[turn, which, side] = jnp.zeros((4 * nx + 32, depth), BF16)
            return c

        lax.fori_loop(0, V + 1, clear_halo, 0)
    publish(0)

    greet(
        nbx,
        nby,
        [
            (bx + dx, jnp.int32(to), both(bx + dx >= 0, bx + dx < nbx, jnp.logical_or(by != to, dx != 0)))
            for dx in (-1, 0, 1)
            for to in range(nby)
        ],
    )
    offer(Eb.at[0], 0, V)
    start_views()

    def split(band):
        high = band.astype(BF16)
        return high, (band - high.astype(F32)).astype(BF16)

    row = lax.broadcasted_iota(jnp.int32, (ny, 128), 0)
    col = lax.broadcasted_iota(jnp.int32, (ny, 128), 1)
    inside = col < ny
    second = col >= ny + 16
    place = jnp.where(inside, col, jnp.where(second, ny + (col & 3), (col & 3) - H))
    owner = jnp.where(inside, -1, (col & 15) >> 2)
    lag_y = place - row + H
    z_in = lax.broadcasted_iota(jnp.int32, (depth, depth), 0)
    z_out = lax.broadcasted_iota(jnp.int32, (depth, depth), 1)
    lag_z = z_in - z_out + (kz - 1) // 2

    def total_of(v, first, length):
        total = taps[v, first]
        for b in range(1, length):
            total = total + taps[v, first + b]
        return total

    def build(v, c):
        scale_xy = 1.0 / jnp.full((ny, 128), total_of(v, 0, kxy) * total_of(v, kxy, kxy), F32)
        scale_z = 1.0 / jnp.full((depth, depth), total_of(v, 2 * kxy, kz), F32)
        forth = jnp.zeros((ny, 128), F32)
        back = jnp.zeros((ny, 128), F32)
        for b in range(kxy):
            forth = jnp.where(lag_y == b, taps[v, kxy + b], forth)
            back = jnp.where(lag_y == b, taps[v, 2 * kxy - 1 - b], back)
        for j in range(4):
            used = jnp.logical_and(
                jnp.logical_or(owner == -1, owner == j), col < ny + 32
            )
            for target, band in ((LF, forth), (LT, back)):
                high, rest = split(jnp.where(used, band * scale_xy, 0.0))
                base = pl.multiple_of(v * ny, ny)
                target[j, pl.ds(base, ny), 0:128] = high
                target[j, pl.ds(base, ny), 128:256] = rest
        forth = jnp.zeros((depth, depth), F32)
        back = jnp.zeros((depth, depth), F32)
        for b in range(kz):
            forth = jnp.where(lag_z == b, taps[v, 2 * kxy + b], forth)
            back = jnp.where(lag_z == b, taps[v, 2 * kxy + kz - 1 - b], back)
        forth = forth * scale_z
        back = back * scale_z
        for target, band in ((ZF, forth), (ZT, back)):
            high, rest = split(band)
            base = pl.multiple_of(v * 3 * depth, 3 * depth)
            target[pl.ds(base, depth)] = high
            target[pl.ds(base + depth, depth)] = high
            target[pl.ds(base + 2 * depth, depth)] = rest
        weight_z = jnp.sum(back, axis=0, keepdims=True)

        def folded(first, shift, limit, base, rows):
            total = jnp.zeros((rows, 128), F32)
            cell = first - H + lax.broadcasted_iota(jnp.int32, (rows, 128), 0)
            for b in range(kxy):
                here = cell + b
                there = here + shift
                good = both(here >= 0, here < limit, there >= 0, there < limit)
                total = total + jnp.where(good, taps[v, base + kxy - 1 - b], 0.0)
            return total

        planes[v] = folded(by * ny, offsets[v, 1], nby * ny, kxy, ny) * scale_xy * weight_z
        WX[v] = folded(bx * nx, offsets[v, 0], nbx * nx, 0, nx)
        return c

    lax.fori_loop(0, V, build, 0)

    pick_row = lax.broadcasted_iota(jnp.int32, (ny, ny + SHIFT), 0)
    pick_col = lax.broadcasted_iota(jnp.int32, (ny, ny + SHIFT), 1)
    for n, shift in enumerate((SHIFT + offsets[1, 1], offsets[2, 1])):
        pick[n] = jnp.where(pick_col == pick_row + shift, 1.0, 0.0).astype(BF16)

    def invert(i, c):
        rows = [WX[v, pl.ds(pl.multiple_of(8 * i, 8), 8)] for v in range(V)]
        for o in range(8):
            weight = rows[0][o : o + 1] * planes[0]
            for v in range(1, V):
                weight = weight + rows[v][o : o + 1] * planes[v]
            inverse[8 * i + o] = 1.0 / weight
        return c

    lax.fori_loop(0, blocks, invert, 0)

    def column(field, turn, which, q, j):
        tile = pl.ds(pl.multiple_of(16 * q, 16), 16)
        once = [
            field[4 * q + j],
            halo[turn, which, 0, tile],
            halo[turn, which, 1, tile],
            jnp.zeros((128 - ny - 32, depth), BF16),
        ]
        return jnp.concatenate(once + once, axis=0)

    def along_x(v, i, reverse, base):
        weights = [taps[v, kxy - 1 - a if reverse else a] for a in range(kxy)]
        for t in range(0, ny, 16):
            halves = []
            for u in (t, t + 8):
                rows = [G[v, 8 * i + k, u : u + 8] for k in range(7 + kxy)]
                sums = []
                for o in range(8):
                    acc = weights[0] * rows[o]
                    for a in range(1, kxy):
                        acc = acc + weights[a] * rows[o + a]
                    sums.append(acc)
                halves.append(sums)
            for o in range(8):
                both_halves = jnp.concatenate([halves[0][o], halves[1][o]], axis=0)
                high, rest = split(both_halves)
                U[v, pl.ds(base + o * ny + t, 16), :depth] = high
                U[v, pl.ds(base + o * ny + t, 16), depth:] = rest

    def sweep(turn, c):
        accept(Eb.at[turn], turn, V)

        def all_views(q, c):
            for j in range(4):
                got = jnp.dot(
                    LF[j], column(Eb.at[turn], turn, V, q, j), preferred_element_type=F32
                )
                for v in range(V):
                    G[v, 4 * q + j] = got[v * ny : (v + 1) * ny]
            return c

        lax.fori_loop(0, (nx + 2 * H) // 4, all_views, 0)

        def back(v):
            accept(Rb.at[turn, v], turn, v)

            def one_view(q, c):
                for j in range(4):
                    G[v, 4 * q + j] = jnp.dot(
                        LT[j, v * ny : (v + 1) * ny],
                        column(Rb.at[turn, v], turn, v, q, j),
                        preferred_element_type=F32,
                    )
                return c

            lax.fori_loop(0, (nx + 2 * H) // 4, one_view, 0)

            def block(i, c):
                along_x(v, i, True, pl.multiple_of(8 * ny * i, 8 * ny))
                return c

            lax.fori_loop(0, blocks, block, 0)

        for v in range(V):
            first_x = {1: offsets[1, 0], 2: SHIFT + offsets[2, 0]}.get(v, 0)

            def ahead(i, c):
                along_x(v, i, False, 0)
                got = jnp.dot(
                    jnp.concatenate([U[v, : 8 * ny], U[v, : 8 * ny, :depth]], axis=1),
                    ZF[3 * v * depth : 3 * (v + 1) * depth],
                    preferred_element_type=F32,
                )
                for o in range(8):
                    D[8 * i + o] = got[o * ny : (o + 1) * ny] + bg[v]
                return c

            lax.fori_loop(0, blocks, ahead, 0)

            @pl.when(turn == 0)
            def _():
                accept_view(v)

            def divide(i, c):
                for o in range(8):
                    if v in (1, 2):
                        seen = jnp.dot(
                            pick[v - 1], regs[v][first_x + 8 * i + o], preferred_element_type=F32
                        )
                    else:
                        seen = regs[v][8 * i + o].astype(F32)
                    value = seen / D[8 * i + o]
                    Rb[turn, v, H + 8 * i + o] = value.astype(BF16)
                    ratio[o] = value
                pack_rim(lambda o: ratio.at[o], turn, v, i)
                return c

            lax.fori_loop(0, blocks, divide, 0)
            offer(Rb.at[turn, v], turn, v)
            if v:
                back(v - 1)
        back(V - 1)

        def update(i, c):
            here = pl.ds(pl.multiple_of(8 * ny * i, 8 * ny), 8 * ny)
            got = jnp.dot(
                jnp.concatenate(
                    [part for v in range(V) for part in (U[v, here], U[v, here, :depth])], axis=1
                ),
                ZT[...],
                preferred_element_type=F32,
            )
            for o in range(8):
                x = 8 * i + o
                E[x] = E[x] * got[o * ny : (o + 1) * ny] * inverse[x]
            return c

        lax.fori_loop(0, blocks, update, 0)

        finish(Eb.at[turn], turn, V)
        for v in range(V):
            finish(Rb.at[turn, v], turn, v)

        @pl.when(turn < ITERS - 1)
        def _():
            publish(turn + 1)
            offer(Eb.at[turn + 1], turn + 1, V)

        return c

    lax.fori_loop(0, ITERS, sweep, 0)
    finish_views()

    def store(i, c):
        out[i] = E[i]
        return c

    lax.fori_loop(0, nx, store, 0)


def local(views, offsets, background, psf_x, psf_y, psf_z, start):
    rows_x, rows_y, depth = start.shape
    nbx = lax.axis_size("bx")
    nby = lax.axis_size("by")
    blk = views.shape[1]
    vmem = pl.BlockSpec(memory_space=pltpu.VMEM)
    smem = pl.BlockSpec(memory_space=pltpu.SMEM)
    anywhere = pl.BlockSpec(memory_space=pl.ANY)
    taps = jnp.concatenate([psf_x, psf_y, psf_z], axis=1)
    tall = rows_x + 2 * H
    small = (rows_x, rows_y, depth)
    large = (rows_x + SHIFT, rows_y + SHIFT, depth)
    return pl.pallas_call(
        functools.partial(deconvolve_kernel, nbx, nby, rows_x, rows_y, blk, depth),
        out_shape=jax.ShapeDtypeStruct(start.shape, F32),
        in_specs=[anywhere, vmem, smem, smem, smem],
        out_specs=vmem,
        scratch_shapes=[
            pltpu.VMEM(small, BF16),
            pltpu.VMEM(large, BF16),
            pltpu.VMEM(large, BF16),
            pltpu.VMEM(small, BF16),
            pltpu.VMEM(small, F32),
            pltpu.VMEM(small, F32),
            pltpu.VMEM((ITERS, tall, rows_y, depth), BF16),
            pltpu.VMEM((ITERS, V, tall, rows_y, depth), BF16),
            pltpu.VMEM((ITERS, V + 1, 2, H * tall, depth), BF16),
            pltpu.VMEM((ITERS, V + 1, 2, H * rows_x, depth), BF16),
            pltpu.VMEM((V, tall, rows_y, depth), F32),
            pltpu.VMEM((V, rows_x * rows_y, 2 * depth), BF16),
            pltpu.VMEM(small, F32),
            pltpu.VMEM((8, rows_y, depth), F32),
            pltpu.VMEM((2, 32, depth), F32),
            pltpu.VMEM((4, V * rows_y, 256), BF16),
            pltpu.VMEM((4, V * rows_y, 256), BF16),
            pltpu.VMEM((3 * V * depth, depth), BF16),
            pltpu.VMEM((3 * V * depth, depth), BF16),
            pltpu.VMEM((2, rows_y, rows_y + SHIFT), BF16),
            pltpu.VMEM((V, rows_y, depth), F32),
            pltpu.VMEM((V, rows_x, depth), F32),
            pltpu.SemaphoreType.DMA((V, 3, nby)),
            pltpu.SemaphoreType.DMA((V, nby + SHIFT // blk)),
            pltpu.SemaphoreType.DMA((ITERS, V + 1, 8)),
            pltpu.SemaphoreType.DMA((ITERS, V + 1, 8)),
        ],
        compiler_params=pltpu.CompilerParams(
            collective_id=0, has_side_effects=True, vmem_limit_bytes=60 * 1024 * 1024
        ),
    )(views, start, taps, offsets, background)


def solution(mesh):
    return jax.shard_map(
        local,
        mesh=mesh,
        in_specs=(P(None, ("bx", "by"), None, None), P(), P(), P(), P(), P(), P("bx", "by", None)),
        out_specs=P("bx", "by", None),
        check_vma=False,
    )
```
